32 devices in a mesh: row: 8 (over z, core), col: 4 (over y, x).
Axes of the slice: x: 2, y: 2, z: 4, core: 2. Of those that a mesh axis runs over, the one named last changes fastest.
Arguments:
- moment_one: float32 [1536, 6144], P('row', 'col'), may hold values from -40 to 40
- gradient_one: bfloat16 [1536, 6144], P('row', 'col'), may hold values from -6 to 6
- factor_one: float32 [6144, 384], P(('col', 'row')), may hold values from -6 to 6
- moment_two: float32 [1536, 6144], P('row', 'col'), may hold values from -40 to 40
- gradient_two: bfloat16 [1536, 6144], P('row', 'col'), may hold values from -6 to 6
- factor_two: float32 [1536, 384], P(('row', 'col')), may hold values from -6 to 6
Outputs:
- carried_one: float32 [1536, 6144], P('row', 'col')
- right_next: float32 [6144, 384], P(('col', 'row'))
- carried_two: float32 [1536, 6144], P('row', 'col')
- left_next: float32 [1536, 384], P(('row', 'col'))
The draws below stay inside these ranges and needn't reach their ends.
All inputs are finite; a program needn't handle non-finite values.
Results may differ from the reference program's by a relative error of at most 0.0003.
Values sent between devices are 32-bit elements; how exact they have to be, the bound alone decides.
No kernel may reach another device: no remote copies, remote signals or barrier semaphores. Data moves between devices by JAX's collectives and lax.ppermute only.
A program may use at most 64 MiB of HBM per device.

```python
import math
import jax
import jax.numpy as jnp
from jax import lax

N = 6144
RANK = 384
ROWS = 1536


def scaled_matrix(key):
    key_base, key_rows, key_cols = jax.random.split(key, 3)
    rise_rows = jnp.arange(ROWS, dtype=jnp.float32) / ROWS
    rise_cols = jnp.arange(N, dtype=jnp.float32) / N
    base = jnp.clip(jax.random.normal(key_base, (ROWS, N), jnp.float32), -4.0, 4.0)
    row_scale = 0.3 * jnp.exp(math.log(3.0) * rise_rows) * jnp.exp(jax.random.uniform(key_rows, (ROWS,), jnp.float32, 0.0, math.log(3.3)))
    col_scale = 0.3 * jnp.exp(math.log(3.0) * rise_cols) * jnp.exp(jax.random.uniform(key_cols, (N,), jnp.float32, 0.0, math.log(3.3)))
    return base * row_scale[:, None] * col_scale[None, :]


def draw_moment_one(key, part):
    return scaled_matrix(jax.random.fold_in(key, 11))


def draw_moment_two(key, part):
    return scaled_matrix(jax.random.fold_in(key, 23))


def block_scale(key, dims, cuts, least, largest):
    def one(axis_at, shards_of):
        steps = jax.random.uniform(jax.random.fold_in(jax.random.fold_in(key, 6), axis_at), (shards_of,), jnp.float32, least / len(cuts), largest / len(cuts))
        return jnp.repeat(jnp.exp(steps), dims[axis_at] // shards_of).reshape((-1,) + (1,) * (len(dims) - axis_at - 1))

    factor_of = one(*cuts[0])
    for cut in cuts[1:]:
        factor_of = factor_of * one(*cut)
    return factor_of


def bell_draw(rng, dims, scale, reach, shards=(), held_as=jnp.bfloat16):
    values = scale * jax.random.normal(rng, dims, jnp.float32)
    if shards:
        values = values * block_scale(rng, dims, shards, -0.22, 0.18)
    return jnp.clip(values, -reach, reach).astype(held_as)


def setup_inputs(seed: int = 0) -> dict:
    splits = jax.random.split(jax.random.key(seed), 7)
    return {
        "moment_one": draw_moment_one(jax.random.fold_in(splits[6], 71), 0),
        "gradient_one": bell_draw(splits[1], (ROWS, N), 1.0, 6.0, ((0, 8), (1, 4))),
        "factor_one": bell_draw(splits[2], (N, RANK), 1.0, 6.0, ((0, 32),), jnp.float32),
        "moment_two": draw_moment_two(jax.random.fold_in(splits[6], 71), 0),
        "gradient_two": bell_draw(splits[4], (ROWS, N), 1.0, 6.0, ((0, 8), (1, 4))),
        "factor_two": bell_draw(splits[5], (ROWS, RANK), 1.0, 6.0, ((0, 32),), jnp.float32),
    }


momentum_decay = 0.95
epsilon = 1e-06
highest = lax.Precision.HIGHEST

def product_plain(left, right):
    return jnp.dot(left.astype(jnp.float32), right.astype(jnp.float32), precision=highest, preferred_element_type=jnp.float32)

def orthonormal(panel):
    gram = product_plain(panel.T, panel)
    lower = jnp.linalg.cholesky(gram)
    return lax.linalg.triangular_solve(lower, panel, left_side=False, lower=True, transpose_a=True)

def unit_columns(matrix):
    return matrix * lax.rsqrt(lax.optimization_barrier(jnp.mean(matrix * matrix, axis=0)) + epsilon)

def reference(moment_one, gradient_one, factor_one, moment_two, gradient_two, factor_two):
    buffer_one = moment_one + gradient_one.astype(jnp.float32)
    basis_one = orthonormal(product_plain(buffer_one, factor_one))
    right_sum = product_plain(buffer_one.T, basis_one)
    carried_one = buffer_one - (1.0 - momentum_decay) * product_plain(basis_one, right_sum.T)
    right_next = unit_columns(right_sum)
    buffer_two = moment_two + gradient_two.astype(jnp.float32)
    basis_two = orthonormal(product_plain(buffer_two.T, factor_two))
    left_sum = product_plain(buffer_two, basis_two)
    carried_two = buffer_two - (1.0 - momentum_decay) * product_plain(left_sum, basis_two.T)
    left_next = unit_columns(left_sum)
    return (carried_one, right_next, carried_two, left_next)
```

```python
import functools

import jax
import jax.numpy as jnp
from jax import lax
from jax.experimental import pallas as pl
from jax.experimental.pallas import tpu as pltpu
from jax.sharding import PartitionSpec as P

momentum_decay = 0.95
epsilon = 1e-06
highest = lax.Precision.HIGHEST
tile = 128


def product(left, right, over_left, over_right, precision=highest):
    return lax.dot_general(
        left,
        right,
        (((over_left,), (over_right,)), ((), ())),
        precision=precision,
        preferred_element_type=jnp.float32,
    )


def eliminate(blocks):
    lane = lax.broadcasted_iota(jnp.int32, (8, tile), 1)
    sub = lax.broadcasted_iota(jnp.int32, (8, tile), 0)
    count = tile // 8
    work = [[block[8 * i : 8 * i + 8, :] for i in range(count)] for block in blocks]
    for j in range(tile):
        t, s = divmod(j, 8)
        for rows in work:
            inverse = 1.0 / rows[t][s : s + 1, j : j + 1]
            pivot = jnp.where(lane[:1] == j, 1.0, rows[t][s : s + 1, :]) * inverse
            pivot = jnp.broadcast_to(pivot, (8, tile))
            for i in range(t, count):
                column = jnp.broadcast_to(rows[i][:, j : j + 1], (8, tile))
                hit = lane == j
                if i == t:
                    if s == 7:
                        continue
                    column = jnp.where(sub > s, column, 0.0)
                    hit = hit & (sub > s)
                rows[i] = jnp.where(hit, 0.0, rows[i]) - column * pivot
    outs = []
    for rows in work:
        out = []
        for i in range(count):
            row = sub + 8 * i
            diagonal = jnp.sum(jnp.where(lane == row, rows[i], 0.0), axis=1, keepdims=True)
            scale = lax.rsqrt(diagonal)
            scale = scale * (1.5 - 0.5 * diagonal * scale * scale)
            out.append(jnp.where(lane < row, rows[i], jnp.where(lane == row, 1.0, 0.0)) * scale)
        outs.append(jnp.concatenate(out, axis=0))
    return outs


def inverse_kernel(*refs):
    count = len(refs) // 2
    grams, outs = refs[:count], refs[count:]
    blocks = grams[0].shape[0] // tile
    at = lambda i: slice(tile * i, tile * i + tile)
    every = range(count)
    rest = [{(i, j): g[at(i), at(j)] for i in range(blocks) for j in range(i + 1)} for g in grams]
    diagonal = [{} for _ in every]
    lower = [{} for _ in every]
    for b in range(blocks):
        found = eliminate([rest[m][b, b] for m in every])
        for m in every:
            diagonal[m][b] = found[m]
            for i in range(b + 1, blocks):
                lower[m][i, b] = product(rest[m][i, b], found[m], 1, 1)
            for i in range(b + 1, blocks):
                for j in range(b + 1, i + 1):
                    rest[m][i, j] = rest[m][i, j] - product(lower[m][i, b], lower[m][j, b], 1, 1)
    for m in every:
        inverse = {}
        for i in range(blocks):
            inverse[i, i] = diagonal[m][i]
            for j in range(i):
                total = product(lower[m][i, j], inverse[j, j], 1, 0)
                for k in range(j + 1, i):
                    total = total + product(lower[m][i, k], inverse[k, j], 1, 0)
                inverse[i, j] = -product(diagonal[m][i], total, 1, 0)
        for i in range(blocks):
            for j in range(blocks):
                outs[m][at(i), at(j)] = inverse[i, j] if j <= i else jnp.zeros((tile, tile), jnp.float32)


def inverse_factors(*grams):
    whole = pl.BlockSpec(memory_space=pltpu.VMEM)
    return pl.pallas_call(
        inverse_kernel,
        out_shape=tuple(jax.ShapeDtypeStruct(g.shape, jnp.float32) for g in grams),
        in_specs=[whole] * len(grams),
        out_specs=tuple(whole for _ in grams),
        compiler_params=pltpu.CompilerParams(vmem_limit_bytes=32 * 2**20),
        cost_estimate=pl.CostEstimate(flops=10**9, bytes_accessed=10**7, transcendentals=0),
    )(*grams)


def swap_core(x):
    return lax.ppermute(x, "row", [(i, i ^ 1) for i in range(lax.axis_size("row"))])


def move_line(x, step, senders):
    return lax.ppermute(x, "row", [(2 * z + k, 2 * (z + step) + k) for z in senders for k in range(2)])


def turn_line(x, step):
    line = lax.axis_size("row") // 2
    return lax.ppermute(x, "row", [(2 * z + k, 2 * ((z + step) % line) + k) for z in range(line) for k in range(2)])


def swap_col(x, bits):
    return lax.ppermute(x, "col", [(i, i ^ bits) for i in range(lax.axis_size("col"))])


def halves(x):
    half = x.shape[0] // 2
    return x[:half], x[half:]


def gather_line(x, parts=2):
    line = lax.axis_size("row") // 2
    pieces = jnp.split(x, parts, axis=0)
    up, down = [list(pieces)], [list(pieces)]
    for s in range(1, line):
        up.append([move_line(p, 1, range(s - 1, line - 1)) for p in up[-1]])
        down.append([move_line(p, -1, range(1, line - s + 1)) for p in down[-1]])
    return [list(pieces)] + [[u + d for u, d in zip(up[s], down[line - s])] for s in range(1, line)]


def gather_row(x):
    line = lax.axis_size("row") // 2
    me = lax.axis_index("row")
    z, core = me // 2, me % 2
    rows = x.shape[0]
    out = jnp.zeros((2 * line * rows,) + x.shape[1:], x.dtype)
    for s, pieces in enumerate(gather_line(x)):
        offset = 0
        for piece in pieces:
            other = swap_core(piece)
            start = 2 * ((z - s) % line) * rows + offset
            out = lax.dynamic_update_slice(out, piece, (start + core * rows, 0))
            out = lax.dynamic_update_slice(out, other, (start + (1 - core) * rows, 0))
            offset += piece.shape[0]
    return out


def scatter_row(x, parts=2):
    line = lax.axis_size("row") // 2
    me = lax.axis_index("row")
    z, core = me // 2, me % 2
    rows = x.shape[0] // (2 * line)
    x = x.reshape((line, 2, rows) + x.shape[1:])
    keep = lax.dynamic_index_in_dim(x, core, 1, keepdims=False)
    give = lax.dynamic_index_in_dim(x, 1 - core, 1, keepdims=False)
    x = keep + swap_core(give)
    outs = []
    for part in jnp.split(x, parts, axis=1):
        own = lambda at: lax.dynamic_index_in_dim(part, jnp.clip(at, 0, line - 1), 0, keepdims=False)
        up = own(z + line - 1)
        down = own(z - line + 1)
        for s in range(1, line):
            up = move_line(up, 1, range(0, s))
            down = move_line(down, -1, range(line - s, line))
            if s < line - 1:
                up = up + own(z + line - s - 1)
                down = down + own(z - line + s + 1)
        outs.append(own(z) + up + down)
    return jnp.concatenate(outs, axis=0)


def sum_col(x):
    bits = [1 << b for b in range((lax.axis_size("col") - 1).bit_length())]
    low, high = halves(x)
    for up, down in zip(bits, bits[::-1]):
        low, high = low + swap_col(low, up), high + swap_col(high, down)
    return jnp.concatenate((low, high), axis=0)


def gather_col(x):
    me = lax.axis_index("col")
    rows = x.shape[0]
    out = jnp.zeros((lax.axis_size("col") * rows,) + x.shape[1:], x.dtype)
    for bits in range(lax.axis_size("col")):
        piece = swap_col(x, bits) if bits else x
        out = lax.dynamic_update_slice(out, piece, ((me ^ bits) * rows, 0))
    return out


def scatter_col(x):
    me = lax.axis_index("col")
    count = lax.axis_size("col")
    rows = x.shape[0] // count
    own = lambda at: lax.dynamic_slice_in_dim(x, at * rows, rows, 0)
    total = own(me)
    for bits in range(1, count):
        total = total + swap_col(own(me ^ bits), bits)
    return total


def sum_stripe(stripe):
    line = lax.axis_size("row") // 2
    core = lax.axis_index("row") % 2
    rows = stripe.shape[0] // 2
    own = lambda at: lax.dynamic_slice_in_dim(stripe, at * rows, rows, 0)
    part = own(core) + swap_core(own(1 - core))
    moved = [turn_line(part, s) for s in range(1, line)]
    part = functools.reduce(jnp.add, moved, part)
    mine = gather_col(part)
    other = swap_core(mine)
    count = lax.axis_size("col")
    mine = mine.reshape(count, 1, rows, -1)
    other = other.reshape(count, 1, rows, -1)
    first, second = jnp.where(core == 0, mine, other), jnp.where(core == 0, other, mine)
    return jnp.concatenate((first, second), axis=1).reshape(2 * rows * count, -1)


def shards(moment_one, gradient_one, factor_one, moment_two, gradient_two, factor_two):
    col = lax.axis_index("col")
    cols = lax.axis_size("col")
    line = lax.axis_size("row") // 2
    buffer_one = moment_one + gradient_one.astype(jnp.float32)
    buffer_two = moment_two + gradient_two.astype(jnp.float32)
    local_rows, local_cols = buffer_one.shape
    total_cols = local_cols * cols
    total_rows = local_rows * lax.axis_size("row")

    factor_one = gather_row(factor_one)
    factor_two = gather_col(factor_two)
    panel_one = sum_col(product(buffer_one, factor_one, 1, 0))
    panel_two_part = scatter_row(product(buffer_two, factor_two, 0, 0))
    panel_two = gather_row(panel_two_part)

    gram_one = product(panel_one, panel_one, 0, 0)
    stripe = gram_one.shape[0] // cols
    gram_one = sum_stripe(lax.dynamic_slice_in_dim(gram_one, col * stripe, stripe, 0))
    gram_two = sum_stripe(scatter_col(product(panel_two_part, panel_two_part, 0, 0)))

    right_part = scatter_row(product(buffer_one, panel_one, 0, 0))
    right = gather_row(right_part)
    left = sum_col(product(buffer_two, panel_two, 1, 0))

    inverse_one, inverse_two = inverse_factors(gram_one, gram_two)

    right_sum = product(right, inverse_one, 1, 1)
    left_sum = product(left, inverse_two, 1, 1)
    squares_right = jnp.sum(right_sum * right_sum, axis=0, keepdims=True)
    squares_left = jnp.sum(left_sum * left_sum, axis=0, keepdims=True)
    moved = [swap_col(squares_right, b) for b in range(1, cols)]
    squares_right = functools.reduce(jnp.add, moved, squares_right)
    squares_left = squares_left + swap_core(squares_left)
    moved = [turn_line(squares_left, s) for s in range(1, line)]
    squares_left = functools.reduce(jnp.add, moved, squares_left)

    factor = 1.0 - momentum_decay
    weight_one = product(product(panel_one, inverse_one, 1, 1), inverse_one, 1, 0)
    weight_two = product(left_sum, inverse_two, 1, 0)
    carried_one = buffer_one - factor * product(weight_one, right, 1, 1)
    carried_two = buffer_two - factor * product(weight_two, panel_two, 1, 1)

    right_part = product(right_part, inverse_one, 1, 1)
    left_rows = left_sum.shape[0] // cols
    left_part = lax.dynamic_slice_in_dim(left_sum, col * left_rows, left_rows, 0)
    right_next = right_part * lax.rsqrt(squares_right / total_cols + epsilon)
    left_next = left_part * lax.rsqrt(squares_left / total_rows + epsilon)
    return (carried_one, right_next, carried_two, left_next)


def solution(mesh):
    in_specs = (
        P("row", "col"),
        P("row", "col"),
        P(("col", "row"), None),
        P("row", "col"),
        P("row", "col"),
        P(("row", "col"), None),
    )
    out_specs = (P("row", "col"), P(("col", "row"), None), P("row", "col"), P(("row", "col"), None))
    return jax.shard_map(shards, mesh=mesh, in_specs=in_specs, out_specs=out_specs, check_vma=False)
```

```python
import functools

import jax
import jax.numpy as jnp
from jax import lax
from jax.experimental import pallas as pl
from jax.experimental.pallas import tpu as pltpu
from jax.sharding import PartitionSpec as P

momentum_decay = 0.95
epsilon = 1e-06
highest = lax.Precision.HIGHEST
tile = 128
lead = 3
chunks = 3
free = pl.CostEstimate(flops=1, bytes_accessed=1, transcendentals=0)


def product(left, right, over_left, over_right, precision=highest):
    return lax.dot_general(
        left,
        right,
        (((over_left,), (over_right,)), ((), ())),
        precision=precision,
        preferred_element_type=jnp.float32,
    )


def split(x):
    high = x.astype(jnp.bfloat16)
    return high, (x - high.astype(jnp.float32)).astype(jnp.bfloat16)


def product_split(left, right, over_left, over_right):
    (a, b), (c, d) = split(left), split(right)
    one = lambda x, y: product(x, y, over_left, over_right, None)
    return one(a, d) + one(b, c) + one(a, c)


class Flow:
    def __init__(self):
        z, core = row_place()
        self.place = jnp.stack((lax.axis_index("col"), z, core)).astype(jnp.int32)
        self.last = ()

    def __call__(self, kernel, outs, *args, scratch=()):
        last = len(self.last)
        whole = pl.BlockSpec(memory_space=pltpu.VMEM)

        def body(*refs):
            kernel(*refs[last:])

        results = pl.pallas_call(
            body,
            out_shape=[jax.ShapeDtypeStruct(shape, jnp.float32) for shape in outs],
            in_specs=[pl.BlockSpec(memory_space=pl.ANY)] * last
            + [pl.BlockSpec(memory_space=pltpu.SMEM)]
            + [whole] * len(args),
            out_specs=[whole] * len(outs),
            scratch_shapes=[pltpu.VMEM(shape, jnp.float32) for shape in scratch],
            compiler_params=pltpu.CompilerParams(vmem_limit_bytes=24 * 2**20),
            cost_estimate=free,
            name=getattr(kernel, "func", kernel).__name__,
        )(*self.last, self.place, *args)
        self.last = (results[-1],)
        return results


class Task:
    def __init__(self, steps):
        self.steps, self.result = steps, None

    def step(self, times=1):
        for _ in range(times):
            if self.steps is not None:
                try:
                    next(self.steps)
                except StopIteration as end:
                    self.steps, self.result = None, end.value
        return self

    def finish(self):
        while self.steps is not None:
            self.step()
        return self.result


def many(start, size):
    return pl.ds(pl.multiple_of(start, tile), size)


def eliminate(blocks):
    lane = lax.broadcasted_iota(jnp.int32, (8, tile), 1)
    sub = lax.broadcasted_iota(jnp.int32, (8, tile), 0)
    count = tile // 8
    work = [[block[8 * i : 8 * i + 8, :] for i in range(count)] for block in blocks]

    def spread(rows, j):
        return {i: jnp.broadcast_to(rows[i][:, j : j + 1], (8, tile)) for i in range(j // 8, count)}

    ahead = [{j: spread(rows, j) for j in range(lead)} for rows in work]
    for j in range(tile):
        t, s = divmod(j, 8)
        for rows, columns in zip(work, ahead):
            if j + lead < tile:
                columns[j + lead] = spread(rows, j + lead)
            column = columns.pop(j)
            inverse = 1.0 / column[t][s : s + 1, :]
            pivot = jnp.where(lane[:1] == j, 1.0, rows[t][s : s + 1, :]) * inverse
            pivot = jnp.broadcast_to(pivot, (8, tile))
            for later, values in columns.items():
                u, v = divmod(later, 8)
                weight = jnp.broadcast_to(column[u][v : v + 1, :] * inverse, (8, tile))
                for i in values:
                    values[i] = values[i] - column[i] * weight
            for i in range(t, count):
                below, hit = column[i], lane == j
                if i == t:
                    if s == 7:
                        continue
                    below = jnp.where(sub > s, below, 0.0)
                    hit = hit & (sub > s)
                rows[i] = jnp.where(hit, 0.0, rows[i]) - below * pivot
    outs = []
    for rows in work:
        out = []
        for i in range(count):
            row = sub + 8 * i
            diagonal = jnp.sum(jnp.where(lane == row, rows[i], 0.0), axis=1, keepdims=True)
            scale = lax.rsqrt(diagonal)
            scale = scale * (1.5 - 0.5 * diagonal * scale * scale)
            out.append(jnp.where(lane < row, rows[i], jnp.where(lane == row, 1.0, 0.0)) * scale)
        outs.append(jnp.concatenate(out, axis=0))
    return outs


def inverse_blocks(grams, outs):
    blocks = grams[0].shape[0] // tile
    at = lambda i: slice(tile * i, tile * i + tile)
    every = range(len(grams))
    rest = [{(i, j): g[at(i), at(j)] for i in range(blocks) for j in range(i + 1)} for g in grams]
    diagonal = [{} for _ in every]
    lower = [{} for _ in every]
    for b in range(blocks):
        found = eliminate([rest[m][b, b] for m in every])
        for m in every:
            diagonal[m][b] = found[m]
            for i in range(b + 1, blocks):
                lower[m][i, b] = product(rest[m][i, b], found[m], 1, 1)
            for i in range(b + 1, blocks):
                for j in range(b + 1, i + 1):
                    rest[m][i, j] = rest[m][i, j] - product(lower[m][i, b], lower[m][j, b], 1, 1)
    for m in every:
        inverse = {}
        for i in range(blocks):
            inverse[i, i] = diagonal[m][i]
            for j in range(i):
                total = product(lower[m][i, j], inverse[j, j], 1, 0)
                for k in range(j + 1, i):
                    total = total + product(lower[m][i, k], inverse[k, j], 1, 0)
                inverse[i, j] = -product(diagonal[m][i], total, 1, 0)
        for i in range(blocks):
            for j in range(blocks):
                outs[m][at(i), at(j)] = inverse[i, j] if j <= i else jnp.zeros((tile, tile), jnp.float32)


def inverse_kernel(place, *refs):
    *stripes, mine, other, out_one, out_two, gram_one, gram_two = refs
    col, core = place[0], place[2]
    rows = stripes[0].shape[0]
    for bits, stripe in enumerate(stripes):
        gram_one[pl.ds(pl.multiple_of((col ^ bits) * rows, 8), rows), :] = stripe[...]
    half = mine.shape[0]
    gram_two[pl.ds(pl.multiple_of(core * half, 8), half), :] = mine[...]
    gram_two[pl.ds(pl.multiple_of((1 - core) * half, 8), half), :] = other[...]
    inverse_blocks((gram_one, gram_two), (out_one, out_two))


def rows_of(refs):
    return jnp.concatenate([r[...] for r in refs], axis=0)


def half_buffer(moment, gradient, core, half):
    at = many(core * half, half)
    return moment[:, at] + gradient[:, at].astype(jnp.float32)


def give_kernel(place, moment, gradient, *refs):
    *parts, out = refs
    buffer = half_buffer(moment, gradient, 1 - place[2], out.shape[0])
    out[...] = product_split(buffer, rows_of(parts), 0, 0)


def keep_kernel(count, place, moment, gradient, came, *refs):
    parts, outs = refs[:count], refs[count:]
    half = came.shape[0]
    rows = half // len(outs)
    value = product_split(half_buffer(moment, gradient, place[2], half), rows_of(parts), 0, 0) + came[...]
    for i, out in enumerate(outs):
        out[...] = value[i * rows : (i + 1) * rows]


def add_kernel(place, *refs):
    count = len(refs) // 3
    for i in range(count):
        refs[2 * count + i][...] = refs[2 * i][...] + refs[2 * i + 1][...]


def total_kernel(place, *refs):
    *parts, out = refs
    total = parts[0][...]
    for part in parts[1:]:
        total = total + part[...]
    out[...] = total


def pick_kernel(low, high, place, x, moved, out):
    ends = (place[1] == low) | (place[1] == high)
    out[...] = jnp.where(ends, moved[...], x[...])


def order_kernel(place, mine, other, out):
    first = place[2] == 0
    a, b = mine[...], other[...]
    out[...] = jnp.concatenate((jnp.where(first, a, b), jnp.where(first, b, a)), axis=0)


def stack_kernel(place, own, *refs):
    *moved, out = refs
    count = len(moved) // 2
    up, down = moved[:count], moved[count:]
    rows = own.shape[0]
    out[:rows, :] = own[...]
    for s in range(1, count + 1):
        out[s * rows : (s + 1) * rows, :] = up[count - s][...] + down[s - 1][...]


def first_panel(line, place, moment, gradient, mine, other, low, high):
    width = moment.shape[1] // line
    rows = width // 2
    first = place[2] == 0
    total = None
    for s in range(line):
        at = many(lax.rem(place[1] + s, line) * width, width)
        buffer = moment[:, at] + gradient[:, at].astype(jnp.float32)
        a, b = mine[s * rows : (s + 1) * rows, :], other[s * rows : (s + 1) * rows, :]
        factor = jnp.concatenate((jnp.where(first, a, b), jnp.where(first, b, a)), axis=0)
        term = product_split(buffer, factor, 1, 0)
        total = term if total is None else total + term
    half = low.shape[0]
    low[...] = total[:half]
    high[...] = total[half:]


def stripe_kernel(place, low, high, keep, give, gram):
    panel = rows_of((low, high))
    gram[...] = product(panel, panel, 0, 0)
    half = keep.shape[0]
    stripe = gram[pl.ds(pl.multiple_of(place[0] * 2 * half, 8), 2 * half), :]
    first = place[2] == 0
    keep[...] = jnp.where(first, stripe[:half], stripe[half:])
    give[...] = jnp.where(first, stripe[half:], stripe[:half])


def gram_kernel(place, *refs):
    *parts, keep, give = refs
    panel = rows_of(parts)
    gram = product(panel, panel, 0, 0)
    half = keep.shape[0]
    first = place[2] == 0
    keep[...] = jnp.where(first, gram[:half], gram[half:])
    give[...] = jnp.where(first, gram[half:], gram[:half])


def second_product(count, place, moment, gradient, *refs):
    mine, other, (low, high) = refs[:count], refs[count : 2 * count], refs[2 * count :]
    total = None
    for core, parts in ((place[2], mine), (1 - place[2], other)):
        panel = rows_of(parts)
        at = many(core * panel.shape[0], panel.shape[0])
        term = product_split(moment[:, at] + gradient[:, at].astype(jnp.float32), panel, 1, 0)
        total = term if total is None else total + term
    half = low.shape[0]
    low[...] = total[:half]
    high[...] = total[half:]


def right_kernel(count, place, *refs):
    mine, other, (inverse, out, squares) = refs[:count], refs[count : 2 * count], refs[2 * count :]
    total = None
    for core, parts in ((place[2], mine), (1 - place[2], other)):
        value = product_split(rows_of(parts), inverse[...], 1, 1)
        out[pl.ds(pl.multiple_of(core * value.shape[0], 8), value.shape[0]), :] = value
        term = jnp.sum(value * value, axis=0, keepdims=True)
        total = term if total is None else total + term
    squares[...] = total


def left_kernel(place, low, high, inverse, out, weight, squares):
    value = product_split(rows_of((low, high)), inverse[...], 1, 1)
    out[...] = value
    weight[...] = product_split(value, inverse[...], 1, 0)
    squares[...] = jnp.sum(value * value, axis=0, keepdims=True)


def carry(moment, gradient, at, weight, panel, out):
    change = product_split(weight, panel, 1, 1)
    out[:, at] = moment[:, at] + gradient[:, at].astype(jnp.float32) - (1.0 - momentum_decay) * change


def carry_one_kernel(place, moment, gradient, low, high, inverse, right, out):
    weight = product_split(rows_of((low, high)), inverse[...], 1, 1)
    step = right.shape[0] // 2
    for i in range(2):
        at = pl.ds(i * step, step)
        carry(moment, gradient, at, weight, right[at, :], out)


def carry_two_kernel(count, place, moment, gradient, *refs):
    mine, other, (weight, out) = refs[:count], refs[count : 2 * count], refs[2 * count :]
    for core, parts in ((place[2], mine), (1 - place[2], other)):
        panel = rows_of(parts)
        at = many(core * panel.shape[0], panel.shape[0])
        carry(moment, gradient, at, weight[...], panel, out)


def line_size():
    return lax.axis_size("row") // 2


def row_place():
    me = lax.axis_index("row")
    return me // 2, me % 2


def swap_core(x):
    return lax.ppermute(x, "row", [(i, i ^ 1) for i in range(lax.axis_size("row"))])


def move_line(x, pairs):
    return lax.ppermute(x, "row", [(2 * a + k, 2 * b + k) for a, b in pairs for k in range(2)])


def turn_line(x, step):
    line = line_size()
    return move_line(x, [(z, (z + step) % line) for z in range(line)])


def swap_col(x, bits):
    return lax.ppermute(x, "col", [(i, i ^ bits) for i in range(lax.axis_size("col"))])


def gather_line(flow, x):
    line = line_size()
    up, down = [x], [x]
    for s in range(1, line):
        up.append(move_line(up[-1], [(z, z + 1) for z in range(s - 1, line - 1)]))
        down.append(move_line(down[-1], [(z, z - 1) for z in range(1, line - s + 1)]))
    mine = flow(stack_kernel, [(line * x.shape[0], x.shape[1])], *up, *down[1:])[0]
    return mine, swap_core(mine)


def sum_line(flow, x):
    line = line_size()
    half = line // 2
    for h in range(half - 1):
        moved = move_line(x, [(h, h + 1), (line - 1 - h, line - 2 - h)])
        yield
        x = flow(add_kernel, [x.shape], x, moved)[0]
    moved = move_line(x, [(half - 1, half), (half, half - 1)])
    yield
    x = flow(add_kernel, [x.shape], x, moved)[0]
    for h in range(half - 2, -1, -1):
        moved = move_line(x, [(h + 1, h), (line - 2 - h, line - 1 - h)])
        yield
        x = flow(functools.partial(pick_kernel, h, line - 1 - h), [x.shape], x, moved)[0]
    return x, swap_core(x)


def col_bits():
    return [1 << b for b in range((lax.axis_size("col") - 1).bit_length())]


def sum_col(flow, low, high):
    bits = col_bits()
    for up, down in zip(bits, bits[::-1]):
        moved = swap_col(low, up), swap_col(high, down)
        yield
        low, high = flow(add_kernel, [low.shape, high.shape], low, moved[0], high, moved[1])
    return low, high


def gather_col(x):
    me = lax.axis_index("col")
    rows = x.shape[0]
    out = jnp.zeros((lax.axis_size("col") * rows,) + x.shape[1:], x.dtype)
    for bits in range(lax.axis_size("col")):
        piece = swap_col(x, bits) if bits else x
        out = lax.dynamic_update_slice(out, piece, ((me ^ bits) * rows, 0))
    return out


def rows_at(x, start, rows):
    return lax.dynamic_slice_in_dim(x, start, rows, 0)


def gram_stripes(flow, low, high):
    cols = lax.axis_size("col")
    size = low.shape[1]
    shape = (size // (2 * cols), size)
    keep, give = flow(stripe_kernel, [shape, shape], low, high, scratch=[(size, size)])
    moved = swap_core(give)
    yield
    part = flow(add_kernel, [shape], keep, moved)[0]
    moved = [turn_line(part, s) for s in range(1, line_size())]
    yield
    part = flow(total_kernel, [shape], part, *moved)[0]
    moved = swap_core(part)
    yield
    stripe = flow(order_kernel, [(2 * shape[0], size)], part, moved)[0]
    return [stripe] + [swap_col(stripe, bits) for bits in range(1, cols)]


def gram_halves(flow, parts):
    size = parts[0].shape[1]
    shape = (size // 2, size)
    part, give = flow(gram_kernel, [shape, shape], *parts)
    moved = swap_core(give)
    yield
    part = flow(add_kernel, [shape], part, moved)[0]
    for bits in col_bits():
        moved = swap_col(part, bits)
        yield
        part = flow(add_kernel, [shape], part, moved)[0]
    return [part, swap_core(part)]


def sum_squares(flow, right, left):
    moved = [swap_col(right, b) for b in range(1, lax.axis_size("col"))]
    came = swap_core(left)
    yield
    left = flow(add_kernel, [left.shape], left, came)[0]
    turned = [turn_line(left, s) for s in range(1, line_size())]
    yield
    return functools.reduce(jnp.add, moved, right), functools.reduce(jnp.add, turned, left)


def shards(moment_one, gradient_one, factor_one, moment_two, gradient_two, factor_two):
    flow = Flow()
    col = lax.axis_index("col")
    cols = lax.axis_size("col")
    line = line_size()
    one, two = (moment_one, gradient_one), (moment_two, gradient_two)
    local_rows, local_cols = moment_one.shape
    rank = factor_one.shape[1]
    total_cols = local_cols * cols
    total_rows = local_rows * lax.axis_size("row")
    half = (local_cols // 2, rank)
    chunk = (half[0] // chunks, rank)
    low_high = [(local_rows // 2, rank)] * 2
    block = (local_rows, rank)
    square = (rank, rank)

    def transposed(buffer, *parts):
        came = swap_core(flow(give_kernel, [half], *buffer, *parts)[0])
        yield
        kernel = functools.partial(keep_kernel, len(parts))
        values = flow(kernel, [chunk] * chunks, *buffer, came, *parts)
        return [Task(sum_line(flow, value)).step() for value in values]

    panel_two = Task(transposed(two, gather_col(factor_two))).step().finish()

    factor = gather_line(flow, factor_one)
    panel_one = flow(functools.partial(first_panel, line), low_high, *one, *factor)
    panel_one = Task(sum_col(flow, *panel_one)).step()
    panel_two[0].step()
    panel_one.step()
    panel_two[1].step()
    panel_one = panel_one.finish()

    right = Task(transposed(one, *panel_one)).step()
    gram_one = Task(gram_stripes(flow, *panel_one)).step()
    right = right.finish()
    gram_one.step()
    panel_two[2].step()
    panel_two[0].step()
    panel_two[1].step()
    gram_one.step()
    right[0].step()
    panel_two[2].step()
    gram_one = gram_one.finish()
    panel_two[0].finish()
    right[1].step()
    panel_two[1].finish()
    right[2].step()
    panel_two[2].finish()

    panel_two = [part for task in panel_two for part in task.result]
    panel_two = panel_two[::2] + panel_two[1::2]
    gram_two = Task(gram_halves(flow, panel_two[:chunks])).step(2)
    left = flow(functools.partial(second_product, chunks), low_high, *two, *panel_two)
    left = Task(sum_col(flow, *left)).step()
    right[0].step()
    gram_two.step()
    left.step()
    right[1].step()
    gram_two = gram_two.finish()
    left = left.finish()
    right[2].step()

    inverse_one, inverse_two = flow(
        inverse_kernel, [square, square], *gram_one, *gram_two, scratch=[square, square]
    )
    right = [part for task in right for part in task.finish()]
    right = right[::2] + right[1::2]

    left_sum, weight_two, squares_left = flow(left_kernel, [block, block, (1, rank)], *left, inverse_two)
    kernel = functools.partial(right_kernel, chunks)
    right_sum, squares_right = flow(kernel, [(local_cols, rank), (1, rank)], *right, inverse_one)
    squares = Task(sum_squares(flow, squares_right, squares_left)).step(2)
    kernel = functools.partial(carry_two_kernel, chunks)
    carried_two = flow(kernel, [moment_two.shape], *two, *panel_two, weight_two)[0]
    carried_one = flow(carry_one_kernel, [moment_one.shape], *one, *panel_one, inverse_one, right_sum)[0]
    squares_right, squares_left = squares.finish()

    right_rows = local_cols // (2 * line)
    right_part = rows_at(right_sum, lax.axis_index("row") * right_rows, right_rows)
    left_rows = local_rows // cols
    left_part = rows_at(left_sum, col * left_rows, left_rows)
    right_next = right_part * lax.rsqrt(squares_right / total_cols + epsilon)
    left_next = left_part * lax.rsqrt(squares_left / total_rows + epsilon)
    return (carried_one, right_next, carried_two, left_next)


def solution(mesh):
    in_specs = (
        P("row", "col"),
        P("row", "col"),
        P(("col", "row"), None),
        P("row", "col"),
        P("row", "col"),
        P(("row", "col"), None),
    )
    out_specs = (P("row", "col"), P(("col", "row"), None), P("row", "col"), P(("row", "col"), None))
    return jax.shard_map(shards, mesh=mesh, in_specs=in_specs, out_specs=out_specs, check_vma=False)
```

```python
import functools

import jax
import jax.numpy as jnp
from jax import lax
from jax.experimental import pallas as pl
from jax.experimental.pallas import tpu as pltpu
from jax.sharding import PartitionSpec as P

momentum_decay = 0.95
epsilon = 1e-06
highest = lax.Precision.HIGHEST
tile = 128
lead = 3
chunks = 3
free = pl.CostEstimate(flops=1, bytes_accessed=1, transcendentals=0)


def product(left, right, over_left, over_right, precision=highest):
    return lax.dot_general(
        left,
        right,
        (((over_left,), (over_right,)), ((), ())),
        precision=precision,
        preferred_element_type=jnp.float32,
    )


def split(x):
    high = x.astype(jnp.bfloat16)
    return high, (x - high.astype(jnp.float32)).astype(jnp.bfloat16)


def product_split(left, right, over_left, over_right):
    (a, b), (c, d) = split(left), split(right)
    one = lambda x, y: product(x, y, over_left, over_right, None)
    return one(a, d) + one(b, c) + one(a, c)


class Flow:
    def __init__(self):
        z, core = row_place()
        self.place = jnp.stack((lax.axis_index("col"), z, core)).astype(jnp.int32)
        self.last = ()

    def __call__(self, kernel, outs, *args, scratch=(), wait=()):
        waits = self.last + tuple(wait)
        last = len(waits)
        whole = pl.BlockSpec(memory_space=pltpu.VMEM)

        def body(*refs):
            kernel(*refs[last:])

        results = pl.pallas_call(
            body,
            out_shape=[jax.ShapeDtypeStruct(shape, jnp.float32) for shape in outs],
            in_specs=[pl.BlockSpec(memory_space=pl.ANY)] * last
            + [pl.BlockSpec(memory_space=pltpu.SMEM)]
            + [whole] * len(args),
            out_specs=[whole] * len(outs),
            scratch_shapes=[pltpu.VMEM(shape, jnp.float32) for shape in scratch],
            compiler_params=pltpu.CompilerParams(vmem_limit_bytes=16 * 2**20),
            cost_estimate=free,
            name=getattr(kernel, "func", kernel).__name__,
        )(*waits, self.place, *args)
        self.last = (results[-1],)
        return results


class Task:
    def __init__(self, steps):
        self.steps, self.result = steps, None

    def step(self, times=1):
        for _ in range(times):
            if self.steps is not None:
                try:
                    next(self.steps)
                except StopIteration as end:
                    self.steps, self.result = None, end.value
        return self

    def finish(self):
        while self.steps is not None:
            self.step()
        return self.result


def many(start, size):
    return pl.ds(pl.multiple_of(start, tile), size)


def eliminate(blocks):
    lane = lax.broadcasted_iota(jnp.int32, (8, tile), 1)
    sub = lax.broadcasted_iota(jnp.int32, (8, tile), 0)
    count = tile // 8
    work = [[block[8 * i : 8 * i + 8, :] for i in range(count)] for block in blocks]

    def spread(rows, j):
        return {i: jnp.broadcast_to(rows[i][:, j : j + 1], (8, tile)) for i in range(j // 8, count)}

    ahead = [{j: spread(rows, j) for j in range(lead)} for rows in work]
    for j in range(tile):
        t, s = divmod(j, 8)
        for rows, columns in zip(work, ahead):
            if j + lead < tile:
                columns[j + lead] = spread(rows, j + lead)
            column = columns.pop(j)
            inverse = 1.0 / column[t][s : s + 1, :]
            pivot = jnp.where(lane[:1] == j, 1.0, rows[t][s : s + 1, :]) * inverse
            pivot = jnp.broadcast_to(pivot, (8, tile))
            for later, values in columns.items():
                u, v = divmod(later, 8)
                weight = jnp.broadcast_to(column[u][v : v + 1, :] * inverse, (8, tile))
                for i in values:
                    values[i] = values[i] - column[i] * weight
            for i in range(t, count):
                below, hit = column[i], lane == j
                if i == t:
                    if s == 7:
                        continue
                    below = jnp.where(sub > s, below, 0.0)
                    hit = hit & (sub > s)
                rows[i] = jnp.where(hit, 0.0, rows[i]) - below * pivot
    outs = []
    for rows in work:
        out = []
        for i in range(count):
            row = sub + 8 * i
            diagonal = jnp.sum(jnp.where(lane == row, rows[i], 0.0), axis=1, keepdims=True)
            scale = lax.rsqrt(diagonal)
            scale = scale * (1.5 - 0.5 * diagonal * scale * scale)
            out.append(jnp.where(lane < row, rows[i], jnp.where(lane == row, 1.0, 0.0)) * scale)
        outs.append(jnp.concatenate(out, axis=0))
    return outs


def inverse_blocks(grams, outs):
    blocks = grams[0].shape[0] // tile
    at = lambda i: slice(tile * i, tile * i + tile)
    every = range(len(grams))
    rest = [{(i, j): g[at(i), at(j)] for i in range(blocks) for j in range(i + 1)} for g in grams]
    diagonal = [{} for _ in every]
    lower = [{} for _ in every]
    for b in range(blocks):
        found = eliminate([rest[m][b, b] for m in every])
        for m in every:
            diagonal[m][b] = found[m]
            for i in range(b + 1, blocks):
                lower[m][i, b] = product(rest[m][i, b], found[m], 1, 1)
            for i in range(b + 1, blocks):
                for j in range(b + 1, i + 1):
                    rest[m][i, j] = rest[m][i, j] - product(lower[m][i, b], lower[m][j, b], 1, 1)
    for m in every:
        inverse = {}
        for i in range(blocks):
            inverse[i, i] = diagonal[m][i]
            for j in range(i):
                total = product(lower[m][i, j], inverse[j, j], 1, 0)
                for k in range(j + 1, i):
                    total = total + product(lower[m][i, k], inverse[k, j], 1, 0)
                inverse[i, j] = -product(diagonal[m][i], total, 1, 0)
        for i in range(blocks):
            for j in range(blocks):
                outs[m][at(i), at(j)] = inverse[i, j] if j <= i else jnp.zeros((tile, tile), jnp.float32)


def gather_kernel(place, *refs):
    *stripes, out = refs
    rows = stripes[0].shape[0]
    for bits, stripe in enumerate(stripes):
        out[pl.ds(pl.multiple_of((place[0] ^ bits) * rows, 8), rows), :] = stripe[...]


def inverse_kernel(place, gram_one, mine, other, out_one, out_two, gram_two):
    half = mine.shape[0]
    gram_two[pl.ds(pl.multiple_of(place[2] * half, 8), half), :] = mine[...]
    gram_two[pl.ds(pl.multiple_of((1 - place[2]) * half, 8), half), :] = other[...]
    inverse_blocks((gram_one, gram_two), (out_one, out_two))


def rows_of(refs):
    return jnp.concatenate([r[...] for r in refs], axis=0)


def half_buffer(moment, gradient, core, half):
    at = many(core * half, half)
    return moment[:, at] + gradient[:, at].astype(jnp.float32)


def give_kernel(place, moment, gradient, *refs):
    *parts, out = refs
    buffer = half_buffer(moment, gradient, 1 - place[2], out.shape[0])
    out[...] = product_split(buffer, rows_of(parts), 0, 0)


def keep_kernel(count, place, moment, gradient, came, *refs):
    parts, outs = refs[:count], refs[count:]
    half = came.shape[0]
    rows = half // len(outs)
    value = product_split(half_buffer(moment, gradient, place[2], half), rows_of(parts), 0, 0) + came[...]
    for i, out in enumerate(outs):
        out[...] = value[i * rows : (i + 1) * rows]


def add_kernel(place, *refs):
    count = len(refs) // 3
    for i in range(count):
        refs[2 * count + i][...] = refs[2 * i][...] + refs[2 * i + 1][...]


def total_kernel(place, *refs):
    *parts, out = refs
    total = parts[0][...]
    for part in parts[1:]:
        total = total + part[...]
    out[...] = total


def pick_kernel(low, high, place, x, moved, out):
    ends = (place[1] == low) | (place[1] == high)
    out[...] = jnp.where(ends, moved[...], x[...])


def order_kernel(place, mine, other, out):
    first = place[2] == 0
    a, b = mine[...], other[...]
    out[...] = jnp.concatenate((jnp.where(first, a, b), jnp.where(first, b, a)), axis=0)


def first_panel(line, place, moment, gradient, *refs):
    mine, other, (low, high) = refs[:line], refs[line : 2 * line], refs[2 * line :]
    width = moment.shape[1] // line
    first = place[2] == 0
    total = None
    for s in range(line):
        at = many(lax.rem(place[1] + s, line) * width, width)
        buffer = moment[:, at] + gradient[:, at].astype(jnp.float32)
        a, b = mine[s][...], other[s][...]
        factor = jnp.concatenate((jnp.where(first, a, b), jnp.where(first, b, a)), axis=0)
        term = product_split(buffer, factor, 1, 0)
        total = term if total is None else total + term
    half = low.shape[0]
    low[...] = total[:half]
    high[...] = total[half:]


def stripe_kernel(place, low, high, keep, give, gram):
    panel = rows_of((low, high))
    gram[...] = product(panel, panel, 0, 0)
    half = keep.shape[0]
    stripe = gram[pl.ds(pl.multiple_of(place[0] * 2 * half, 8), 2 * half), :]
    first = place[2] == 0
    keep[...] = jnp.where(first, stripe[:half], stripe[half:])
    give[...] = jnp.where(first, stripe[half:], stripe[:half])


def gram_kernel(place, *refs):
    *parts, keep, give = refs
    panel = rows_of(parts)
    gram = product(panel, panel, 0, 0)
    half = keep.shape[0]
    first = place[2] == 0
    keep[...] = jnp.where(first, gram[:half], gram[half:])
    give[...] = jnp.where(first, gram[half:], gram[:half])


def second_product(count, place, moment, gradient, *refs):
    mine, other, (low, high) = refs[:count], refs[count : 2 * count], refs[2 * count :]
    total = None
    for core, parts in ((place[2], mine), (1 - place[2], other)):
        panel = rows_of(parts)
        at = many(core * panel.shape[0], panel.shape[0])
        term = product_split(moment[:, at] + gradient[:, at].astype(jnp.float32), panel, 1, 0)
        total = term if total is None else total + term
    half = low.shape[0]
    low[...] = total[:half]
    high[...] = total[half:]


def right_kernel(count, place, *refs):
    mine, other, (inverse, out, squares) = refs[:count], refs[count : 2 * count], refs[2 * count :]
    total = None
    for core, parts in ((place[2], mine), (1 - place[2], other)):
        value = product_split(rows_of(parts), inverse[...], 1, 1)
        out[pl.ds(pl.multiple_of(core * value.shape[0], 8), value.shape[0]), :] = value
        term = jnp.sum(value * value, axis=0, keepdims=True)
        total = term if total is None else total + term
    squares[...] = total


def left_kernel(place, low, high, inverse, out, weight, squares):
    value = product_split(rows_of((low, high)), inverse[...], 1, 1)
    out[...] = value
    weight[...] = product_split(value, inverse[...], 1, 0)
    squares[...] = jnp.sum(value * value, axis=0, keepdims=True)


def carry(moment, gradient, at, weight, panel, out):
    change = product_split(weight, panel, 1, 1)
    out[:, at] = moment[:, at] + gradient[:, at].astype(jnp.float32) - (1.0 - momentum_decay) * change


def carry_one_kernel(place, moment, gradient, low, high, inverse, right, out):
    weight = product_split(rows_of((low, high)), inverse[...], 1, 1)
    step = right.shape[0] // 2
    for i in range(2):
        at = pl.ds(i * step, step)
        carry(moment, gradient, at, weight, right[at, :], out)


def carry_two_kernel(count, place, moment, gradient, *refs):
    mine, other, (weight, out) = refs[:count], refs[count : 2 * count], refs[2 * count :]
    for core, parts in ((place[2], mine), (1 - place[2], other)):
        panel = rows_of(parts)
        at = many(core * panel.shape[0], panel.shape[0])
        carry(moment, gradient, at, weight[...], panel, out)


def line_size():
    return lax.axis_size("row") // 2


def row_place():
    me = lax.axis_index("row")
    return me // 2, me % 2


def swap_core(x):
    return lax.ppermute(x, "row", [(i, i ^ 1) for i in range(lax.axis_size("row"))])


def move_line(x, pairs):
    return lax.ppermute(x, "row", [(2 * a + k, 2 * b + k) for a, b in pairs for k in range(2)])


def turn_line(x, step):
    line = line_size()
    return move_line(x, [(z, (z + step) % line) for z in range(line)])


def swap_col(x, bits):
    return lax.ppermute(x, "col", [(i, i ^ bits) for i in range(lax.axis_size("col"))])


def gather_line(flow, x):
    line = line_size()
    up, down, mine, other = [x], [x], {0: x}, {0: swap_core(x)}
    for s in range(1, line):
        up.append(move_line(up[-1], [(z, z + 1) for z in range(s - 1, line - 1)]))
        down.append(move_line(down[-1], [(z, z - 1) for z in range(1, line - s + 1)]))
        yield up[-1], down[-1]
        ready = [k for k in range(1, line) if max(k, line - k) == s]
        if ready:
            pairs = [y for k in ready for y in (up[line - k], down[k])]
            for k, y in zip(ready, flow(add_kernel, [x.shape] * len(ready), *pairs)):
                mine[k], other[k] = y, swap_core(y)
    return [mine[k] for k in range(line)] + [other[k] for k in range(line)]


def sum_line(flow, x):
    line = line_size()
    half = line // 2
    for h in range(half - 1):
        moved = move_line(x, [(h, h + 1), (line - 1 - h, line - 2 - h)])
        yield
        x = flow(add_kernel, [x.shape], x, moved)[0]
    moved = move_line(x, [(half - 1, half), (half, half - 1)])
    yield
    x = flow(add_kernel, [x.shape], x, moved)[0]
    for h in range(half - 2, -1, -1):
        moved = move_line(x, [(h + 1, h), (line - 2 - h, line - 1 - h)])
        yield
        x = flow(functools.partial(pick_kernel, h, line - 1 - h), [x.shape], x, moved)[0]
    return x, swap_core(x)


def col_bits():
    return [1 << b for b in range((lax.axis_size("col") - 1).bit_length())]


def sum_col(flow, low, high):
    bits = col_bits()
    for up, down in zip(bits, bits[::-1]):
        moved = swap_col(low, up), swap_col(high, down)
        yield
        low, high = flow(add_kernel, [low.shape, high.shape], low, moved[0], high, moved[1])
    return low, high


def gather_col(x):
    me = lax.axis_index("col")
    rows = x.shape[0]
    out = jnp.zeros((lax.axis_size("col") * rows,) + x.shape[1:], x.dtype)
    for bits in range(lax.axis_size("col")):
        piece = swap_col(x, bits) if bits else x
        out = lax.dynamic_update_slice(out, piece, ((me ^ bits) * rows, 0))
    return out


def rows_at(x, start, rows):
    return lax.dynamic_slice_in_dim(x, start, rows, 0)


def gram_stripes(flow, low, high):
    cols = lax.axis_size("col")
    size = low.shape[1]
    shape = (size // (2 * cols), size)
    keep, give = flow(stripe_kernel, [shape, shape], low, high, scratch=[(size, size)])
    moved = swap_core(give)
    yield
    part = flow(add_kernel, [shape], keep, moved)[0]
    moved = [turn_line(part, s) for s in range(1, line_size())]
    yield
    part = flow(total_kernel, [shape], part, *moved)[0]
    moved = swap_core(part)
    yield
    stripe = flow(order_kernel, [(2 * shape[0], size)], part, moved)[0]
    moved = [swap_col(stripe, bits) for bits in range(1, cols)]
    yield
    return flow(gather_kernel, [(size, size)], stripe, *moved)[0]


def gram_halves(flow, parts):
    size = parts[0].shape[1]
    shape = (size // 2, size)
    part, give = flow(gram_kernel, [shape, shape], *parts)
    moved = swap_core(give)
    yield
    part = flow(add_kernel, [shape], part, moved)[0]
    for bits in col_bits():
        moved = swap_col(part, bits)
        yield
        part = flow(add_kernel, [shape], part, moved)[0]
    return [part, swap_core(part)]


def sum_left(flow, left):
    came = swap_core(left)
    yield
    left = flow(add_kernel, [left.shape], left, came)[0]
    turned = [turn_line(left, s) for s in range(1, line_size())]
    yield
    return flow(total_kernel, [left.shape], left, *turned)[0]


def sum_right(flow, right):
    moved = [swap_col(right, b) for b in range(1, lax.axis_size("col"))]
    yield
    return flow(total_kernel, [right.shape], right, *moved)[0]


def shards(moment_one, gradient_one, factor_one, moment_two, gradient_two, factor_two):
    flow = Flow()
    col = lax.axis_index("col")
    cols = lax.axis_size("col")
    line = line_size()
    one, two = (moment_one, gradient_one), (moment_two, gradient_two)
    local_rows, local_cols = moment_one.shape
    rank = factor_one.shape[1]
    total_cols = local_cols * cols
    total_rows = local_rows * lax.axis_size("row")
    half = (local_cols // 2, rank)
    chunk = (half[0] // chunks, rank)
    low_high = [(local_rows // 2, rank)] * 2
    block = (local_rows, rank)
    square = (rank, rank)

    def transposed(buffer, *parts, wait=()):
        came = swap_core(flow(give_kernel, [half], *buffer, *parts, wait=wait)[0])
        yield
        kernel = functools.partial(keep_kernel, len(parts))
        values = flow(kernel, [chunk] * chunks, *buffer, came, *parts)
        return [Task(sum_line(flow, value)).step() for value in values]

    gather = gather_line(flow, factor_one)
    came = next(gather)
    factor = Task(gather).step()
    panel_two = Task(transposed(two, gather_col(factor_two), wait=came)).step()
    panel_two = panel_two.finish()
    factor.step()
    panel_two[0].step()
    factor = factor.finish()

    panel_one = flow(functools.partial(first_panel, line), low_high, *one, *factor)
    panel_one = Task(sum_col(flow, *panel_one)).step()
    panel_two[1].step()
    panel_one.step()
    panel_two[2].step()
    panel_two[0].step()
    panel_one = panel_one.finish()

    gram_one = Task(gram_stripes(flow, *panel_one)).step()
    right = Task(transposed(one, *panel_one)).step()
    gram_one.step()
    right = right.finish()
    panel_two[1].step()
    panel_two[0].finish()
    gram_one.step()
    panel_two[2].step()
    gram_one.step()
    right[0].step()
    panel_two[1].finish()
    gram_one = gram_one.finish()
    panel_two[2].finish()
    right[1].step()

    panel_two = [part for task in panel_two for part in task.result]
    panel_two = panel_two[::2] + panel_two[1::2]
    gram_two = Task(gram_halves(flow, panel_two[:chunks])).step(2)
    left = flow(functools.partial(second_product, chunks), low_high, *two, *panel_two)
    left = Task(sum_col(flow, *left)).step()
    right[0].step()
    right[2].step()
    gram_two.step()
    left.step()
    right[1].step()
    gram_two = gram_two.finish()
    left = left.finish()
    right[2].step()

    inverse_one, inverse_two = flow(inverse_kernel, [square, square], gram_one, *gram_two, scratch=[square])

    for task in right:
        task.finish()
    left_sum, weight_two, squares_left = flow(left_kernel, [block, block, (1, rank)], *left, inverse_two)
    squares_left = Task(sum_left(flow, squares_left)).step()
    right = [part for task in right for part in task.result]
    right = right[::2] + right[1::2]
    kernel = functools.partial(right_kernel, chunks)
    right_sum, squares_right = flow(kernel, [(local_cols, rank), (1, rank)], *right, inverse_one)
    squares_right = Task(sum_right(flow, squares_right)).step()
    squares_left.step()
    kernel = functools.partial(carry_two_kernel, chunks)
    carried_two = flow(kernel, [moment_two.shape], *two, *panel_two, weight_two)[0]
    squares_right = squares_right.finish()
    carried_one = flow(carry_one_kernel, [moment_one.shape], *one, *panel_one, inverse_one, right_sum)[0]
    squares_left = squares_left.finish()

    right_rows = local_cols // (2 * line)
    right_part = rows_at(right_sum, lax.axis_index("row") * right_rows, right_rows)
    left_rows = local_rows // cols
    left_part = rows_at(left_sum, col * left_rows, left_rows)
    right_next = right_part * lax.rsqrt(squares_right / total_cols + epsilon)
    left_next = left_part * lax.rsqrt(squares_left / total_rows + epsilon)
    return (carried_one, right_next, carried_two, left_next)


def solution(mesh):
    in_specs = (
        P("row", "col"),
        P("row", "col"),
        P(("col", "row"), None),
        P("row", "col"),
        P("row", "col"),
        P(("row", "col"), None),
    )
    out_specs = (P("row", "col"), P(("col", "row"), None), P("row", "col"), P(("row", "col"), None))
    return jax.shard_map(shards, mesh=mesh, in_specs=in_specs, out_specs=out_specs, check_vma=False)
```

```python
import functools

import jax
import jax.numpy as jnp
from jax import lax
from jax.experimental import pallas as pl
from jax.experimental.pallas import tpu as pltpu
from jax.sharding import PartitionSpec as P

momentum_decay = 0.95
epsilon = 1e-06
highest = lax.Precision.HIGHEST
tile = 128
lead = 3
chunks = 3
free = pl.CostEstimate(flops=1, bytes_accessed=1, transcendentals=0)


def product(left, right, over_left, over_right, precision=highest):
    return lax.dot_general(
        left,
        right,
        (((over_left,), (over_right,)), ((), ())),
        precision=precision,
        preferred_element_type=jnp.float32,
    )


def split(x):
    high = x.astype(jnp.bfloat16)
    return high, (x - high.astype(jnp.float32)).astype(jnp.bfloat16)


def product_split(left, right, over_left, over_right):
    (a, b), (c, d) = split(left), split(right)
    one = lambda x, y: product(x, y, over_left, over_right, None)
    return one(a, d) + one(b, c) + one(a, c)


class Flow:
    def __init__(self):
        z, core = row_place()
        self.place = jnp.stack((lax.axis_index("col"), z, core)).astype(jnp.int32)
        self.last = ()

    def __call__(self, kernel, outs, *args, scratch=(), wait=()):
        waits = self.last + tuple(wait)
        last = len(waits)
        whole = pl.BlockSpec(memory_space=pltpu.VMEM)

        def body(*refs):
            kernel(*refs[last:])

        results = pl.pallas_call(
            body,
            out_shape=[jax.ShapeDtypeStruct(shape, jnp.float32) for shape in outs],
            in_specs=[pl.BlockSpec(memory_space=pl.ANY)] * last
            + [pl.BlockSpec(memory_space=pltpu.SMEM)]
            + [whole] * len(args),
            out_specs=[whole] * len(outs),
            scratch_shapes=[pltpu.VMEM(shape, jnp.float32) for shape in scratch],
            compiler_params=pltpu.CompilerParams(vmem_limit_bytes=16 * 2**20),
            cost_estimate=free,
            name=getattr(kernel, "func", kernel).__name__,
        )(*waits, self.place, *args)
        self.last = (results[-1],)
        return results


class Task:
    def __init__(self, steps):
        self.steps, self.result = steps, None

    def step(self, times=1):
        for _ in range(times):
            if self.steps is not None:
                try:
                    next(self.steps)
                except StopIteration as end:
                    self.steps, self.result = None, end.value
        return self

    def finish(self):
        while self.steps is not None:
            self.step()
        return self.result


def many(start, size):
    return pl.ds(pl.multiple_of(start, tile), size)


def eliminate(blocks):
    lane = lax.broadcasted_iota(jnp.int32, (8, tile), 1)
    sub = lax.broadcasted_iota(jnp.int32, (8, tile), 0)
    count = tile // 8
    work = [[block[8 * i : 8 * i + 8, :] for i in range(count)] for block in blocks]

    def spread(rows, j):
        return {i: jnp.broadcast_to(rows[i][:, j : j + 1], (8, tile)) for i in range(j // 8, count)}

    ahead = [{j: spread(rows, j) for j in range(lead)} for rows in work]
    for j in range(tile):
        t, s = divmod(j, 8)
        for rows, columns in zip(work, ahead):
            if j + lead < tile:
                columns[j + lead] = spread(rows, j + lead)
            column = columns.pop(j)
            inverse = 1.0 / column[t][s : s + 1, :]
            pivot = jnp.where(lane[:1] == j, 1.0, rows[t][s : s + 1, :]) * inverse
            pivot = jnp.broadcast_to(pivot, (8, tile))
            for later, values in columns.items():
                u, v = divmod(later, 8)
                weight = jnp.broadcast_to(column[u][v : v + 1, :] * inverse, (8, tile))
                for i in values:
                    values[i] = values[i] - column[i] * weight
            for i in range(t, count):
                below, hit = column[i], lane == j
                if i == t:
                    if s == 7:
                        continue
                    below = jnp.where(sub > s, below, 0.0)
                    hit = hit & (sub > s)
                rows[i] = jnp.where(hit, 0.0, rows[i]) - below * pivot
    outs = []
    for rows in work:
        out = []
        for i in range(count):
            row = sub + 8 * i
            diagonal = jnp.sum(jnp.where(lane == row, rows[i], 0.0), axis=1, keepdims=True)
            scale = lax.rsqrt(diagonal)
            scale = scale * (1.5 - 0.5 * diagonal * scale * scale)
            out.append(jnp.where(lane < row, rows[i], jnp.where(lane == row, 1.0, 0.0)) * scale)
        outs.append(jnp.concatenate(out, axis=0))
    return outs


def inverse_blocks(grams, outs):
    blocks = grams[0].shape[0] // tile
    at = lambda i: slice(tile * i, tile * i + tile)
    every = range(len(grams))
    rest = [{(i, j): g[at(i), at(j)] for i in range(blocks) for j in range(i + 1)} for g in grams]
    diagonal = [{} for _ in every]
    lower = [{} for _ in every]
    for b in range(blocks):
        found = eliminate([rest[m][b, b] for m in every])
        for m in every:
            diagonal[m][b] = found[m]
            for i in range(b + 1, blocks):
                lower[m][i, b] = product(rest[m][i, b], found[m], 1, 1)
            for i in range(b + 1, blocks):
                for j in range(b + 1, i + 1):
                    rest[m][i, j] = rest[m][i, j] - product(lower[m][i, b], lower[m][j, b], 1, 1)
    for m in every:
        inverse = {}
        for i in range(blocks):
            inverse[i, i] = diagonal[m][i]
            for j in range(i):
                total = product(lower[m][i, j], inverse[j, j], 1, 0)
                for k in range(j + 1, i):
                    total = total + product(lower[m][i, k], inverse[k, j], 1, 0)
                inverse[i, j] = -product(diagonal[m][i], total, 1, 0)
        for i in range(blocks):
            for j in range(blocks):
                outs[m][at(i), at(j)] = inverse[i, j] if j <= i else jnp.zeros((tile, tile), jnp.float32)


def gather_kernel(place, *refs):
    *stripes, out = refs
    rows = stripes[0].shape[0]
    for bits, stripe in enumerate(stripes):
        out[pl.ds(pl.multiple_of((place[0] ^ bits) * rows, 8), rows), :] = stripe[...]


def inverse_kernel(place, gram_one, *refs):
    *parts, out_one, out_two, gram_two = refs
    half = 2 * parts[0].shape[0]
    gram_two[pl.ds(pl.multiple_of(place[2] * half, 8), half), :] = rows_of(parts[:2])
    gram_two[pl.ds(pl.multiple_of((1 - place[2]) * half, 8), half), :] = rows_of(parts[2:])
    inverse_blocks((gram_one, gram_two), (out_one, out_two))


def rows_of(refs):
    return jnp.concatenate([r[...] for r in refs], axis=0)


def half_buffer(moment, gradient, core, half):
    at = many(core * half, half)
    return moment[:, at] + gradient[:, at].astype(jnp.float32)


def give_kernel(place, moment, gradient, *refs):
    *parts, out = refs
    buffer = half_buffer(moment, gradient, 1 - place[2], out.shape[0])
    out[...] = product_split(buffer, rows_of(parts), 0, 0)


def keep_kernel(count, place, moment, gradient, came, *refs):
    parts, outs = refs[:count], refs[count:]
    half = came.shape[0]
    rows = half // len(outs)
    value = product_split(half_buffer(moment, gradient, place[2], half), rows_of(parts), 0, 0) + came[...]
    for i, out in enumerate(outs):
        out[...] = value[i * rows : (i + 1) * rows]


def add_kernel(place, *refs):
    count = len(refs) // 3
    for i in range(count):
        refs[2 * count + i][...] = refs[2 * i][...] + refs[2 * i + 1][...]


def halve_kernel(place, x, moved, low, high):
    total = x[...] + moved[...]
    half = low.shape[0]
    low[...] = total[:half]
    high[...] = total[half:]


def total_kernel(place, *refs):
    *parts, out = refs
    total = parts[0][...]
    for part in parts[1:]:
        total = total + part[...]
    out[...] = total


def pick_kernel(low, high, place, x, moved, out):
    ends = (place[1] == low) | (place[1] == high)
    out[...] = jnp.where(ends, moved[...], x[...])


def order_kernel(place, mine, other, out):
    first = place[2] == 0
    a, b = mine[...], other[...]
    out[...] = jnp.concatenate((jnp.where(first, a, b), jnp.where(first, b, a)), axis=0)


def first_panel(line, place, moment, gradient, *refs):
    mine, other, (low, high) = refs[:line], refs[line : 2 * line], refs[2 * line :]
    width = moment.shape[1] // line
    first = place[2] == 0
    total = None
    for s in range(line):
        at = many(lax.rem(place[1] + s, line) * width, width)
        buffer = moment[:, at] + gradient[:, at].astype(jnp.float32)
        a, b = mine[s][...], other[s][...]
        factor = jnp.concatenate((jnp.where(first, a, b), jnp.where(first, b, a)), axis=0)
        term = product_split(buffer, factor, 1, 0)
        total = term if total is None else total + term
    half = low.shape[0]
    low[...] = total[:half]
    high[...] = total[half:]


def stripe_kernel(place, low, high, keep, give, gram):
    panel = rows_of((low, high))
    gram[...] = product(panel, panel, 0, 0)
    half = keep.shape[0]
    stripe = gram[pl.ds(pl.multiple_of(place[0] * 2 * half, 8), 2 * half), :]
    first = place[2] == 0
    keep[...] = jnp.where(first, stripe[:half], stripe[half:])
    give[...] = jnp.where(first, stripe[half:], stripe[:half])


def gram_kernel(place, *refs):
    *parts, keep, give = refs
    panel = rows_of(parts)
    gram = product(panel, panel, 0, 0)
    half = keep.shape[0]
    first = place[2] == 0
    keep[...] = jnp.where(first, gram[:half], gram[half:])
    give[...] = jnp.where(first, gram[half:], gram[:half])


def second_product(count, place, moment, gradient, *refs):
    mine, other, (low, high) = refs[:count], refs[count : 2 * count], refs[2 * count :]
    total = None
    for core, parts in ((place[2], mine), (1 - place[2], other)):
        panel = rows_of(parts)
        at = many(core * panel.shape[0], panel.shape[0])
        term = product_split(moment[:, at] + gradient[:, at].astype(jnp.float32), panel, 1, 0)
        total = term if total is None else total + term
    half = low.shape[0]
    low[...] = total[:half]
    high[...] = total[half:]


def right_kernel(count, place, *refs):
    mine, other, (inverse, out, squares) = refs[:count], refs[count : 2 * count], refs[2 * count :]
    total = None
    for core, parts in ((place[2], mine), (1 - place[2], other)):
        value = product_split(rows_of(parts), inverse[...], 1, 1)
        out[pl.ds(pl.multiple_of(core * value.shape[0], 8), value.shape[0]), :] = value
        term = jnp.sum(value * value, axis=0, keepdims=True)
        total = term if total is None else total + term
    squares[...] = total


def left_kernel(place, low, high, inverse, out, weight, squares):
    value = product_split(rows_of((low, high)), inverse[...], 1, 1)
    out[...] = value
    weight[...] = product_split(value, inverse[...], 1, 0)
    squares[...] = jnp.sum(value * value, axis=0, keepdims=True)


def carry(moment, gradient, at, weight, panel, out):
    change = product_split(weight, panel, 1, 1)
    out[:, at] = moment[:, at] + gradient[:, at].astype(jnp.float32) - (1.0 - momentum_decay) * change


def carry_one_kernel(place, moment, gradient, low, high, inverse, right, out):
    weight = product_split(rows_of((low, high)), inverse[...], 1, 1)
    step = right.shape[0] // 2
    for i in range(2):
        at = pl.ds(i * step, step)
        carry(moment, gradient, at, weight, right[at, :], out)


def carry_two_kernel(count, place, moment, gradient, *refs):
    mine, other, (weight, out) = refs[:count], refs[count : 2 * count], refs[2 * count :]
    for core, parts in ((place[2], mine), (1 - place[2], other)):
        panel = rows_of(parts)
        at = many(core * panel.shape[0], panel.shape[0])
        carry(moment, gradient, at, weight[...], panel, out)


def line_size():
    return lax.axis_size("row") // 2


def row_place():
    me = lax.axis_index("row")
    return me // 2, me % 2


def swap_core(x):
    return lax.ppermute(x, "row", [(i, i ^ 1) for i in range(lax.axis_size("row"))])


def move_line(x, pairs):
    return lax.ppermute(x, "row", [(2 * a + k, 2 * b + k) for a, b in pairs for k in range(2)])


def turn_line(x, step):
    line = line_size()
    return move_line(x, [(z, (z + step) % line) for z in range(line)])


def swap_col(x, bits):
    return lax.ppermute(x, "col", [(i, i ^ bits) for i in range(lax.axis_size("col"))])


def gather_line(flow, x):
    line = line_size()
    up, down, mine, other = [x], [x], {0: x}, {0: swap_core(x)}
    for s in range(1, line):
        up.append(move_line(up[-1], [(z, z + 1) for z in range(s - 1, line - 1)]))
        down.append(move_line(down[-1], [(z, z - 1) for z in range(1, line - s + 1)]))
        yield up[-1], down[-1]
        ready = [k for k in range(1, line) if max(k, line - k) == s]
        if ready:
            pairs = [y for k in ready for y in (up[line - k], down[k])]
            for k, y in zip(ready, flow(add_kernel, [x.shape] * len(ready), *pairs)):
                mine[k], other[k] = y, swap_core(y)
    return [mine[k] for k in range(line)] + [other[k] for k in range(line)]


def sum_line(flow, x):
    line = line_size()
    half = line // 2
    for h in range(half - 1):
        moved = move_line(x, [(h, h + 1), (line - 1 - h, line - 2 - h)])
        yield
        x = flow(add_kernel, [x.shape], x, moved)[0]
    moved = move_line(x, [(half - 1, half), (half, half - 1)])
    yield
    x = flow(add_kernel, [x.shape], x, moved)[0]
    for h in range(half - 2, -1, -1):
        moved = move_line(x, [(h + 1, h), (line - 2 - h, line - 1 - h)])
        yield
        x = flow(functools.partial(pick_kernel, h, line - 1 - h), [x.shape], x, moved)[0]
    return x, swap_core(x)


def col_bits():
    return [1 << b for b in range((lax.axis_size("col") - 1).bit_length())]


def sum_col(flow, low, high):
    bits = col_bits()
    for up, down in zip(bits, bits[::-1]):
        moved = swap_col(low, up), swap_col(high, down)
        yield
        low, high = flow(add_kernel, [low.shape, high.shape], low, moved[0], high, moved[1])
    return low, high


def gather_col(x):
    me = lax.axis_index("col")
    rows = x.shape[0]
    out = jnp.zeros((lax.axis_size("col") * rows,) + x.shape[1:], x.dtype)
    for bits in range(lax.axis_size("col")):
        piece = swap_col(x, bits) if bits else x
        out = lax.dynamic_update_slice(out, piece, ((me ^ bits) * rows, 0))
    return out


def rows_at(x, start, rows):
    return lax.dynamic_slice_in_dim(x, start, rows, 0)


def gram_stripes(flow, low, high):
    cols = lax.axis_size("col")
    size = low.shape[1]
    shape = (size // (2 * cols), size)
    keep, give = flow(stripe_kernel, [shape, shape], low, high, scratch=[(size, size)])
    moved = swap_core(give)
    yield
    part = flow(add_kernel, [shape], keep, moved)[0]
    moved = [turn_line(part, s) for s in range(1, line_size())]
    yield
    part = flow(total_kernel, [shape], part, *moved)[0]
    moved = swap_core(part)
    yield
    stripe = flow(order_kernel, [(2 * shape[0], size)], part, moved)[0]
    moved = [swap_col(stripe, bits) for bits in range(1, cols)]
    yield
    return flow(gather_kernel, [(size, size)], stripe, *moved)[0]


def gram_halves(flow, parts):
    size = parts[0].shape[1]
    shape = (size // 2, size)
    part, give = flow(gram_kernel, [shape, shape], *parts)
    moved = swap_core(give)
    yield
    low, high = flow(halve_kernel, [(size // 4, size)] * 2, part, moved)
    low, high = yield from sum_col(flow, low, high)
    return [low, high, swap_core(low), swap_core(high)]


def sum_left(flow, left):
    came = swap_core(left)
    yield
    left = flow(add_kernel, [left.shape], left, came)[0]
    turned = [turn_line(left, s) for s in range(1, line_size())]
    yield
    return flow(total_kernel, [left.shape], left, *turned)[0]


def sum_right(flow, right):
    moved = [swap_col(right, b) for b in range(1, lax.axis_size("col"))]
    yield
    return flow(total_kernel, [right.shape], right, *moved)[0]


def shards(moment_one, gradient_one, factor_one, moment_two, gradient_two, factor_two):
    flow = Flow()
    col = lax.axis_index("col")
    cols = lax.axis_size("col")
    line = line_size()
    one, two = (moment_one, gradient_one), (moment_two, gradient_two)
    local_rows, local_cols = moment_one.shape
    rank = factor_one.shape[1]
    total_cols = local_cols * cols
    total_rows = local_rows * lax.axis_size("row")
    half = (local_cols // 2, rank)
    chunk = (half[0] // chunks, rank)
    low_high = [(local_rows // 2, rank)] * 2
    block = (local_rows, rank)
    square = (rank, rank)

    def transposed(buffer, *parts, wait=()):
        came = swap_core(flow(give_kernel, [half], *buffer, *parts, wait=wait)[0])
        yield
        kernel = functools.partial(keep_kernel, len(parts))
        values = flow(kernel, [chunk] * chunks, *buffer, came, *parts)
        return [Task(sum_line(flow, value)).step() for value in values]

    gather = gather_line(flow, factor_one)
    came = next(gather)
    factor = Task(gather).step()
    panel_two = Task(transposed(two, gather_col(factor_two), wait=came)).step()
    panel_two = panel_two.finish()
    factor.step()
    panel_two[0].step()
    factor = factor.finish()

    panel_one = flow(functools.partial(first_panel, line), low_high, *one, *factor)
    panel_one = Task(sum_col(flow, *panel_one)).step()
    panel_two[1].step()
    panel_one.step()
    panel_two[2].step()
    panel_two[0].step()
    panel_one = panel_one.finish()

    gram_one = Task(gram_stripes(flow, *panel_one)).step()
    right = Task(transposed(one, *panel_one)).step()
    gram_one.step()
    right = right.finish()
    panel_two[1].step()
    panel_two[0].finish()
    gram_one.step()
    panel_two[2].step()
    gram_one.step()
    right[0].step()
    panel_two[1].finish()
    gram_one = gram_one.finish()
    panel_two[2].finish()
    right[1].step()

    panel_two = [part for task in panel_two for part in task.result]
    panel_two = panel_two[::2] + panel_two[1::2]
    gram_two = Task(gram_halves(flow, panel_two[:chunks])).step(2)
    left = flow(functools.partial(second_product, chunks), low_high, *two, *panel_two)
    left = Task(sum_col(flow, *left)).step()
    right[0].step()
    right[2].step()
    gram_two.step()
    left.step()
    right[1].step()
    gram_two = gram_two.finish()
    left = left.finish()
    right[2].step()

    inverse_one, inverse_two = flow(inverse_kernel, [square, square], gram_one, *gram_two, scratch=[square])

    for task in right:
        task.finish()
    left_sum, weight_two, squares_left = flow(left_kernel, [block, block, (1, rank)], *left, inverse_two)
    squares_left = Task(sum_left(flow, squares_left)).step()
    right = [part for task in right for part in task.result]
    right = right[::2] + right[1::2]
    kernel = functools.partial(right_kernel, chunks)
    right_sum, squares_right = flow(kernel, [(local_cols, rank), (1, rank)], *right, inverse_one)
    squares_right = Task(sum_right(flow, squares_right)).step()
    squares_left.step()
    kernel = functools.partial(carry_two_kernel, chunks)
    carried_two = flow(kernel, [moment_two.shape], *two, *panel_two, weight_two)[0]
    squares_right = squares_right.finish()
    carried_one = flow(carry_one_kernel, [moment_one.shape], *one, *panel_one, inverse_one, right_sum)[0]
    squares_left = squares_left.finish()

    right_rows = local_cols // (2 * line)
    right_part = rows_at(right_sum, lax.axis_index("row") * right_rows, right_rows)
    left_rows = local_rows // cols
    left_part = rows_at(left_sum, col * left_rows, left_rows)
    right_next = right_part * lax.rsqrt(squares_right / total_cols + epsilon)
    left_next = left_part * lax.rsqrt(squares_left / total_rows + epsilon)
    return (carried_one, right_next, carried_two, left_next)


def solution(mesh):
    in_specs = (
        P("row", "col"),
        P("row", "col"),
        P(("col", "row"), None),
        P("row", "col"),
        P("row", "col"),
        P(("row", "col"), None),
    )
    out_specs = (P("row", "col"), P(("col", "row"), None), P("row", "col"), P(("row", "col"), None))
    return jax.shard_map(shards, mesh=mesh, in_specs=in_specs, out_specs=out_specs, check_vma=False)
```
